32 devices in a mesh: frames: 8 (over z, y), bins: 4 (over x, core).
Axes of the slice: x: 2, y: 2, z: 4, core: 2. Of those that a mesh axis runs over, the one named last changes fastest.
Arguments:
- spectrum: float32 [16384, 1024], P('frames', 'bins'), may hold values from 0.01 to 4
- sign_bits: int32 [16384], P('frames'), may hold values from 0 to 1
- kept_rows: int32 [4096], replicated, may hold values from 0 to 2047, as said below
- mask: int32 [352, 1024], P(None, 'bins'), may hold values 0 or 1
- w_init: float32 [4096, 352], P('frames'), may hold values from 0.02 to 0.2
- h_init: float32 [352, 1024], P(None, 'bins'), may hold values from 0.02 to 0.2
Outputs:
- activations: float32 [4096, 352], P('frames')
- templates: float32 [352, 1024], P(None, 'bins')
The draws below stay inside these ranges and needn't reach their ends.
Inputs may be any that keep to these rules, and one draw needn't show every extreme that they name: `kept_rows`: rows i * 512 to (i + 1) * 512 - 1 hold distinct positions, so each block of 2048 frames gives exactly 512 distinct sketch rows.
All inputs are finite; a program needn't handle non-finite values. No bound on the sum of `mask` on one device may be relied on, other than what follows from the above.
Results may differ from the reference program's by a relative error of at most 0.0001.
Values sent between devices are 32-bit elements; how exact they have to be, the bound alone decides.
A program may use at most 64 MiB of HBM per device.

```python
import math
import jax
import jax.numpy as jnp
from jax import lax

BINS = 1024
K = 352
M = 4096
F_DEV = 2048
ITERS = 2
FRAMES = 16384
MB = 512
N_FRAMES = 8


def draw_kept_rows(key, part):
    blocks = FRAMES // F_DEV
    scores = jax.random.randint(key, (blocks, F_DEV), 0, 1048576) * F_DEV + jnp.arange(F_DEV, dtype=jnp.int32)[None, :]
    order = jnp.argsort(scores, axis=1, stable=True).astype(jnp.int32)
    chosen = order[:, :MB]
    first_high = (chosen - chosen[:, :1] + F_DEV - 1) % F_DEV
    first_low = (chosen - chosen[:, :1] + F_DEV) % F_DEV
    block_ids = jnp.arange(blocks, dtype=jnp.int32)[:, None]
    chosen = jnp.where(block_ids == 0, first_high, jnp.where(block_ids == 1, first_low, chosen))
    return chosen.reshape(M).astype(jnp.int32)


def touch_ends(drawn, own_key, smallest, largest):
    index_at = [jax.random.randint(jax.random.fold_in(own_key, axis), (), 0, length) for axis, length in enumerate(drawn.shape)]
    widest = drawn.shape.index(max(drawn.shape))
    neighbour = index_at[:widest] + [(index_at[widest] + 1) % drawn.shape[widest]] + index_at[widest + 1:]
    return drawn.at[tuple(index_at)].set(smallest).at[tuple(neighbour)].set(largest)


def levels(key, extent, shards, least, high):
    def one(dim, shards_of):
        steps = jax.random.uniform(jax.random.fold_in(jax.random.fold_in(key, 6), dim), (shards_of,), jnp.float32, least / len(shards), high / len(shards))
        return jnp.repeat(jnp.exp(steps), extent[dim] // shards_of).reshape((-1,) + (1,) * (len(extent) - dim - 1))

    level = one(*shards[0])
    for cut in shards[1:]:
        level = level * one(*cut)
    return level


def setup_inputs(seed: int = 0) -> dict:
    arg_keys = jax.random.split(jax.random.key(seed), 7)
    spectrum = jnp.clip(jnp.exp(math.log(4.0) - 5.9914646 * jax.random.uniform(arg_keys[0], (FRAMES, BINS), jnp.float32) ** levels(arg_keys[0], (FRAMES, BINS), ((0, 8), (1, 4)), -0.2, 0.2)), 0.01, 4.0)
    sign_bits = touch_ends(jax.random.randint(arg_keys[1], (FRAMES,), 0, 2), jax.random.fold_in(arg_keys[1], 1), 0, 1).astype(jnp.int32)
    kept_rows = draw_kept_rows(jax.random.fold_in(arg_keys[6], 71), 0)
    mask = touch_ends((jax.random.randint(arg_keys[3], (K, BINS), 0, 4) < 3).astype(jnp.int32), jax.random.fold_in(arg_keys[3], 1), 0, 1)
    w_init = jnp.clip(jnp.exp(math.log(0.2) - 2.3025851 * jax.random.uniform(arg_keys[4], (M, K), jnp.float32) ** levels(arg_keys[4], (M, K), ((0, 8),), -0.2, 0.2)), 0.02, 0.2)
    h_init = jnp.clip(jnp.exp(math.log(0.2) - 2.3025851 * jax.random.uniform(arg_keys[5], (K, BINS), jnp.float32) ** levels(arg_keys[5], (K, BINS), ((1, 4),), -0.2, 0.2)), 0.02, 0.2)
    return dict(spectrum=spectrum, sign_bits=sign_bits, kept_rows=kept_rows, mask=mask, w_init=w_init, h_init=h_init)


def parity_bits(left, right, width):
    joint = jnp.bitwise_and(left, right)
    total = jnp.zeros(joint.shape, jnp.int32)
    for position in range(width):
        total = jnp.bitwise_xor(total, jnp.bitwise_and(jnp.right_shift(joint, position), 1))
    return total

def hadamard(count):
    index = jnp.arange(count, dtype=jnp.int32)
    bits = parity_bits(index[:, None], index[None, :], max(count.bit_length(), 1))
    return (1 - 2 * bits).astype(jnp.float32)

def reference(spectrum, sign_bits, kept_rows, mask, w_init, h_init):
    damping = 1.0
    signed = spectrum * (1 - 2 * sign_bits).astype(jnp.float32)[:, None]
    blocks = signed.reshape(N_FRAMES, F_DEV, BINS)
    local = jnp.einsum('jl,plb->pjb', hadamard(F_DEV), blocks, precision=lax.Precision.HIGHEST)
    mixed = jnp.einsum('qp,pjb->qjb', hadamard(N_FRAMES), local, precision=lax.Precision.HIGHEST)
    owners = (jnp.arange(M, dtype=jnp.int32) // MB).astype(jnp.int32)
    sketch = mixed[owners, kept_rows.astype(jnp.int32)] / jnp.sqrt(jnp.float32(FRAMES))
    templates = h_init * mask.astype(jnp.float32)
    activations = w_init
    high = lax.Precision.HIGHEST
    for round_index in range(ITERS):
        gram_h = jnp.dot(templates, templates.T, precision=high)
        proj = jnp.dot(sketch, templates.T, precision=high)
        lower = jnp.maximum(-proj, 0.0) + jnp.dot(activations, gram_h, precision=high) + damping
        activations = activations * jnp.sqrt((jnp.maximum(proj, 0.0) + damping) / lower)
        cross = jnp.dot(activations.T, sketch, precision=high)
        gram_w = jnp.dot(activations.T, activations, precision=high)
        lower = jnp.maximum(-cross, 0.0) + jnp.dot(gram_w, templates, precision=high) + damping
        templates = templates * jnp.sqrt((jnp.maximum(cross, 0.0) + damping) / lower)
    return (activations, templates)
```

```python
import jax
import jax.numpy as jnp
import numpy as np
from jax import lax
from jax.sharding import PartitionSpec as P

ITERS = 2
SIDE = 256


def hadamard_np(count):
    table = np.ones((1, 1), np.float32)
    while table.shape[0] < count:
        table = np.block([[table, table], [table, -table]])
    return table


def split_2(value):
    high = lax.reduce_precision(value, 8, 7)
    return high.astype(jnp.bfloat16), (value - high).astype(jnp.bfloat16)


def local_hadamard(signed):
    rows, cols = signed.shape
    side = min(SIDE, rows)
    outer = rows // side
    table = jnp.asarray(hadamard_np(side), jnp.bfloat16)
    blocks = signed.reshape(outer, side, cols)
    high, low = split_2(blocks)
    dims = (((1,), (1,)), ((), ()))
    parts = []
    for index in range(outer):
        value = lax.dot_general(table, high[index], (((1,), (0,)), ((), ())), preferred_element_type=jnp.float32)
        value += lax.dot_general(table, low[index], (((1,), (0,)), ((), ())), preferred_element_type=jnp.float32)
        parts.append(value)
    step = 1
    while step < outer:
        nxt = list(parts)
        for index in range(outer):
            if not index & step:
                nxt[index] = parts[index] + parts[index | step]
                nxt[index | step] = parts[index] - parts[index | step]
        parts = nxt
        step *= 2
    return jnp.concatenate(parts, axis=0)


def body(spectrum, sign_bits, kept_rows, mask, w_init, h_init):
    damping = 1.0
    high = lax.Precision.HIGH
    block_count = lax.axis_size("frames")
    position = lax.axis_index("frames")
    frame_rows, cols = spectrum.shape
    per_block = kept_rows.shape[0] // block_count
    signed = spectrum * (1 - 2 * sign_bits).astype(jnp.float32)[:, None]
    local = local_hadamard(signed)
    value = jnp.take(local, kept_rows, axis=0, mode="clip").reshape(block_count, per_block, cols)
    levels = block_count.bit_length() - 1
    for level in range(levels):
        bit = jnp.bitwise_and(jnp.right_shift(position, level), 1)
        pairs = value.reshape(value.shape[0] // 2, 2, per_block, cols)
        keep = lax.dynamic_index_in_dim(pairs, bit, 1, keepdims=False)
        send = lax.dynamic_index_in_dim(pairs, 1 - bit, 1, keepdims=False)
        size = lax.axis_size("frames")
        got = lax.ppermute(send, "frames", [(i, i ^ 1 << level) for i in range(size)])
        value = jnp.where(bit == 1, got - keep, keep + got)
    sketch = value.reshape(per_block, cols)
    sketch = sketch / jnp.sqrt(jnp.float32(frame_rows * block_count))
    templates = h_init * mask.astype(jnp.float32)
    activations = w_init
    for round_index in range(ITERS):
        gram_h, proj = lax.psum(
            (
                jnp.dot(templates, templates.T, precision=high),
                jnp.dot(sketch, templates.T, precision=high),
            ),
            "bins",
        )
        lower = jnp.maximum(-proj, 0.0) + jnp.dot(activations, gram_h, precision=high) + damping
        activations = activations * jnp.sqrt((jnp.maximum(proj, 0.0) + damping) / lower)
        cross, gram_w = lax.psum(
            (
                jnp.dot(activations.T, sketch, precision=high),
                jnp.dot(activations.T, activations, precision=high),
            ),
            "frames",
        )
        lower = jnp.maximum(-cross, 0.0) + jnp.dot(gram_w, templates, precision=high) + damping
        templates = templates * jnp.sqrt((jnp.maximum(cross, 0.0) + damping) / lower)
    return (activations, templates)


def solution(mesh):
    in_specs = (
        P("frames", "bins"),
        P("frames"),
        P(),
        P(None, "bins"),
        P("frames", None),
        P(None, "bins"),
    )
    out_specs = (P("frames", None), P(None, "bins"))
    return jax.shard_map(body, mesh=mesh, in_specs=in_specs, out_specs=out_specs, check_vma=False)
```

```python
import jax
import jax.numpy as jnp
import numpy as np
from jax import lax
from jax.experimental import pallas as pl
from jax.experimental.pallas import tpu as pltpu
from jax.sharding import PartitionSpec as P

ITERS = 2
SIDE = 256


def hadamard_np(count):
    table = np.ones((1, 1), np.float32)
    while table.shape[0] < count:
        table = np.block([[table, table], [table, -table]])
    return table


def split_2(value):
    high = lax.reduce_precision(value, 8, 7)
    return high.astype(jnp.bfloat16), (value - high).astype(jnp.bfloat16)


def local_hadamard(signed):
    rows, cols = signed.shape
    side = min(SIDE, rows)
    outer = rows // side
    table = jnp.asarray(hadamard_np(side), jnp.bfloat16)
    blocks = signed.reshape(outer, side, cols)
    high, low = split_2(blocks)
    dims = (((1,), (1,)), ((), ()))
    parts = []
    for index in range(outer):
        value = lax.dot_general(table, high[index], (((1,), (0,)), ((), ())), preferred_element_type=jnp.float32)
        value += lax.dot_general(table, low[index], (((1,), (0,)), ((), ())), preferred_element_type=jnp.float32)
        parts.append(value)
    step = 1
    while step < outer:
        nxt = list(parts)
        for index in range(outer):
            if not index & step:
                nxt[index] = parts[index] + parts[index | step]
                nxt[index | step] = parts[index] - parts[index | step]
        parts = nxt
        step *= 2
    return jnp.concatenate(parts, axis=0)


def body(spectrum, sign_bits, kept_rows, mask, w_init, h_init):
    damping = 1.0
    high = lax.Precision.HIGH
    block_count = lax.axis_size("frames")
    position = lax.axis_index("frames")
    frame_rows, cols = spectrum.shape
    per_block = kept_rows.shape[0] // block_count
    signed = spectrum * (1 - 2 * sign_bits).astype(jnp.float32)[:, None]
    local = local_hadamard(signed)
    value = jnp.take(local, kept_rows, axis=0, mode="clip").reshape(block_count, per_block, cols)
    levels = block_count.bit_length() - 1
    for level in range(levels):
        bit = jnp.bitwise_and(jnp.right_shift(position, level), 1)
        pairs = value.reshape(value.shape[0] // 2, 2, per_block, cols)
        keep = lax.dynamic_index_in_dim(pairs, bit, 1, keepdims=False)
        send = lax.dynamic_index_in_dim(pairs, 1 - bit, 1, keepdims=False)
        size = lax.axis_size("frames")
        got = lax.ppermute(send, "frames", [(i, i ^ 1 << level) for i in range(size)])
        value = jnp.where(bit == 1, got - keep, keep + got)
    sketch = value.reshape(per_block, cols)
    sketch = sketch / jnp.sqrt(jnp.float32(frame_rows * block_count))
    templates = h_init * mask.astype(jnp.float32)
    activations = w_init
    for round_index in range(ITERS):
        gram_h, proj = lax.psum(
            (
                jnp.dot(templates, templates.T, precision=high),
                jnp.dot(sketch, templates.T, precision=high),
            ),
            "bins",
        )
        lower = jnp.maximum(-proj, 0.0) + jnp.dot(activations, gram_h, precision=high) + damping
        activations = activations * jnp.sqrt((jnp.maximum(proj, 0.0) + damping) / lower)
        cross, gram_w = lax.psum(
            (
                jnp.dot(activations.T, sketch, precision=high),
                jnp.dot(activations.T, activations, precision=high),
            ),
            "frames",
        )
        lower = jnp.maximum(-cross, 0.0) + jnp.dot(gram_w, templates, precision=high) + damping
        templates = templates * jnp.sqrt((jnp.maximum(cross, 0.0) + damping) / lower)
    return (activations, templates)


MESH = pl.DeviceIdType.MESH
VMEM = pl.BlockSpec(memory_space=pltpu.VMEM)
DMA = pltpu.SemaphoreType.DMA
LIMIT = 48 * 1024 * 1024


def flip(index, mask):
    weight = 1
    result = index
    while weight <= mask:
        if mask & weight:
            result = result + weight - 2 * weight * lax.rem(index // weight, 2)
        weight *= 2
    return result


def greet(devices):
    barrier = pltpu.get_barrier_semaphore()
    for device in devices:
        pl.semaphore_signal(barrier, inc=1, device_id=device, device_id_type=MESH)
    pl.semaphore_wait(barrier, len(devices))


def send(src, dst, send_sem, recv_sem, device):
    copy = pltpu.make_async_remote_copy(
        src_ref=src, dst_ref=dst, send_sem=send_sem, recv_sem=recv_sem, device_id=device, device_id_type=MESH
    )
    copy.start()
    return copy


def sketch_kernel(scale, c_ref, out_ref, got_y, got_z, part, send_sem, recv_sem):
    me, col = lax.axis_index("frames"), lax.axis_index("bins")
    side = (flip(me, 1), col)
    near = (flip(me, 2), col)
    far = (flip(me, 4), col)
    greet([side, near, far])
    copies = {}
    for z in (3, 2, 1, 0):
        copies[z] = send(c_ref.at[2 * z + 1], got_y.at[z], send_sem.at[z], recv_sem.at[z], side)
    copies[3].wait_recv()
    part[0] = c_ref[6] + got_y[3]
    first = send(part.at[0], got_z.at[0], send_sem.at[4], recv_sem.at[4], near)
    copies[2].wait_recv()
    first.wait_recv()
    part[1] = c_ref[4] + got_y[2] + got_z[0]
    second = send(part.at[1], got_z.at[1], send_sem.at[5], recv_sem.at[5], far)
    copies[1].wait_recv()
    part[2] = c_ref[2] + got_y[1]
    third = send(part.at[2], got_z.at[2], send_sem.at[6], recv_sem.at[6], near)
    copies[0].wait_recv()
    third.wait_recv()
    second.wait_recv()
    out_ref[...] = ((c_ref[0] + got_y[0]) + (got_z[2] + got_z[1])) * scale
    for copy in (*copies.values(), first, second, third):
        copy.wait_send()


def sum_sketch(terms, scale):
    _, rows, cols = terms.shape
    f32 = jnp.float32
    return pl.pallas_call(
        lambda *refs: sketch_kernel(scale, *refs),
        out_shape=jax.ShapeDtypeStruct((rows, cols), f32),
        in_specs=[VMEM],
        out_specs=VMEM,
        scratch_shapes=[
            pltpu.VMEM((4, rows, cols), f32),
            pltpu.VMEM((3, rows, cols), f32),
            pltpu.VMEM((3, rows, cols), f32),
            DMA((7,)),
            DMA((7,)),
        ],
        compiler_params=pltpu.CompilerParams(collective_id=0, has_side_effects=True, vmem_limit_bytes=LIMIT),
        name="sum_sketch",
    )(terms)


def bins_kernel(g_ref, p_ref, g_out, p_out, g_core, p_core, g_sum, p_sum, g_chip, p_chip, send_sem, recv_sem):
    row, me = lax.axis_index("frames"), lax.axis_index("bins")
    core = lax.rem(me, 2)
    sibling = (row, flip(me, 1))
    across = (row, flip(me, 2))
    greet([sibling, across])
    g_half, p_half = g_ref.shape[0] // 2, p_ref.shape[0] // 2

    def half(ref, which, size):
        return ref.at[pl.ds(pl.multiple_of(which * size, 8), size)]

    arrays = ((g_ref, g_out, g_core, g_sum, g_chip, g_half), (p_ref, p_out, p_core, p_sum, p_chip, p_half))
    stage_1 = [
        send(half(src, 1 - core, size), got, send_sem.at[k], recv_sem.at[k], sibling)
        for k, (src, _, got, _, _, size) in enumerate(arrays)
    ]
    stage_2 = []
    for k, (src, _, got, total, chip, size) in enumerate(arrays):
        stage_1[k].wait_recv()
        total[...] = half(src, core, size)[...] + got[...]
        stage_2.append(send(total, chip, send_sem.at[2 + k], recv_sem.at[2 + k], across))
    stage_3 = []
    for k, (_, out, _, total, chip, size) in enumerate(arrays):
        stage_2[k].wait_recv()
        mine = half(out, core, size)
        mine[...] = total[...] + chip[...]
        stage_3.append(send(mine, mine, send_sem.at[4 + k], recv_sem.at[4 + k], sibling))
    for copy in stage_3:
        copy.wait_recv()
    for copy in (*stage_1, *stage_2, *stage_3):
        copy.wait_send()


def sum_bins(gram, proj):
    f32 = jnp.float32
    g_half = (gram.shape[0] // 2, gram.shape[1])
    p_half = (proj.shape[0] // 2, proj.shape[1])
    return pl.pallas_call(
        bins_kernel,
        out_shape=(jax.ShapeDtypeStruct(gram.shape, f32), jax.ShapeDtypeStruct(proj.shape, f32)),
        in_specs=[VMEM, VMEM],
        out_specs=(VMEM, VMEM),
        scratch_shapes=[pltpu.VMEM(shape, f32) for _ in range(3) for shape in (g_half, p_half)] + [DMA((6,)), DMA((6,))],
        compiler_params=pltpu.CompilerParams(collective_id=1, has_side_effects=True, vmem_limit_bytes=LIMIT),
        name="sum_bins",
    )(gram, proj)


def frames_kernel(g_ref, c_ref, g_out, c_out, g_got, c_got, send_sem, recv_sem):
    me, col = lax.axis_index("frames"), lax.axis_index("bins")
    others = [7, 6, 5, 4, 3, 2, 1]
    device = {r: (flip(me, r), col) for r in others}
    sibling = (me, flip(col, 1))
    across = (me, flip(col, 2))
    greet([device[r] for r in others] + [sibling, across])
    copies = []
    for r in others:
        copies.append(send(g_ref.at[flip(me, r)], g_got.at[r], send_sem.at[r], recv_sem.at[r], device[r]))
    for r in others:
        copies.append(send(c_ref.at[flip(me, r)], c_got.at[r], send_sem.at[8 + r], recv_sem.at[8 + r], device[r]))
    for copy in copies[:7]:
        copy.wait_recv()
    total = g_ref[me]
    for r in others:
        total = total + g_got[r]
    g_out[col, me] = total
    mine = g_out.at[col, me]
    g_copies = [send(mine, mine, send_sem.at[16 + r], recv_sem.at[16 + r], device[r]) for r in others]
    for copy in copies[7:]:
        copy.wait_recv()
    total = c_ref[me]
    for r in others:
        total = total + c_got[r]
    c_out[me] = total
    mine = c_out.at[me]
    c_copies = [send(mine, mine, send_sem.at[24 + r], recv_sem.at[24 + r], device[r]) for r in others]
    for copy in g_copies:
        copy.wait_recv()
    mine = g_out.at[col]
    to_chip = send(mine, mine, send_sem.at[0], recv_sem.at[0], across)
    to_core = send(mine, mine, send_sem.at[8], recv_sem.at[8], sibling)
    to_chip.wait_recv()
    theirs = g_out.at[flip(col, 2)]
    passed = send(theirs, theirs, send_sem.at[16], recv_sem.at[16], sibling)
    for copy in (to_core, passed, *c_copies):
        copy.wait_recv()
    for copy in (*copies, *g_copies, *c_copies, to_chip, to_core, passed):
        copy.wait_send()


def sum_frames(gram, cross):
    f32 = jnp.float32
    return pl.pallas_call(
        frames_kernel,
        out_shape=(jax.ShapeDtypeStruct((4, *gram.shape), f32), jax.ShapeDtypeStruct(cross.shape, f32)),
        in_specs=[VMEM, VMEM],
        out_specs=(VMEM, VMEM),
        scratch_shapes=[pltpu.VMEM(gram.shape, f32), pltpu.VMEM(cross.shape, f32), DMA((32,)), DMA((32,))],
        compiler_params=pltpu.CompilerParams(collective_id=2, has_side_effects=True, vmem_limit_bytes=LIMIT),
        name="sum_frames",
    )(gram, cross)


def body_8x4(spectrum, sign_bits, kept_rows, mask, w_init, h_init):
    damping = 1.0
    high = lax.Precision.HIGH
    block_count = 8
    position = lax.axis_index("frames")
    column = lax.axis_index("bins")
    frame_rows, cols = spectrum.shape
    per_block = kept_rows.shape[0] // block_count
    parts = w_init.shape[1]
    signed = spectrum * (1 - 2 * sign_bits).astype(jnp.float32)[:, None]
    local = local_hadamard(signed)
    blocks = jnp.bitwise_xor(position, jnp.arange(block_count, dtype=jnp.int32))
    rows = jnp.take(kept_rows.reshape(block_count, per_block), blocks, axis=0, mode="clip")
    odd = parity_bits(position, blocks, 3)
    signs = (1 - 2 * odd).astype(jnp.float32)[:, None, None]
    terms = jnp.take(local, rows.reshape(-1), axis=0, mode="clip").reshape(block_count, per_block, cols) * signs
    sketch = sum_sketch(terms, 1.0 / (frame_rows * block_count) ** 0.5)
    templates = h_init * mask.astype(jnp.float32)
    activations = w_init
    quarter = parts // 4
    for round_index in range(ITERS):
        gram_h, proj = sum_bins(
            jnp.dot(templates, templates.T, precision=high),
            jnp.dot(sketch, templates.T, precision=high),
        )
        lower = jnp.maximum(-proj, 0.0) + jnp.dot(activations, gram_h, precision=high) + damping
        activations = activations * jnp.sqrt((jnp.maximum(proj, 0.0) + damping) / lower)
        own = lax.dynamic_slice_in_dim(activations, column * quarter, quarter, axis=1)
        gram_w, cross = sum_frames(
            jnp.dot(own.T, activations, precision=high).reshape(8, quarter // 8, parts),
            jnp.dot(activations.T, sketch, precision=high).reshape(8, parts // 8, cols),
        )
        gram_w = gram_w.reshape(parts, parts)
        cross = cross.reshape(parts, cols)
        lower = jnp.maximum(-cross, 0.0) + jnp.dot(gram_w, templates, precision=high) + damping
        templates = templates * jnp.sqrt((jnp.maximum(cross, 0.0) + damping) / lower)
    return (activations, templates)


def parity_bits(left, right, width):
    joint = jnp.bitwise_and(left, right)
    total = jnp.zeros(joint.shape, jnp.int32)
    for place in range(width):
        total = jnp.bitwise_xor(total, jnp.bitwise_and(jnp.right_shift(joint, place), 1))
    return total


def solution(mesh):
    in_specs = (
        P("frames", "bins"),
        P("frames"),
        P(),
        P(None, "bins"),
        P("frames", None),
        P(None, "bins"),
    )
    out_specs = (P("frames", None), P(None, "bins"))
    small = mesh.shape["frames"] == 8 and mesh.shape["bins"] == 4
    return jax.shard_map(body_8x4 if small else body, mesh=mesh, in_specs=in_specs, out_specs=out_specs, check_vma=False)
```

```python
import jax
import jax.numpy as jnp
import numpy as np
from jax import lax
from jax.experimental import pallas as pl
from jax.experimental.pallas import tpu as pltpu
from jax.sharding import PartitionSpec as P

ITERS = 2
SIDE = 256


def hadamard_np(count):
    table = np.ones((1, 1), np.float32)
    while table.shape[0] < count:
        table = np.block([[table, table], [table, -table]])
    return table


def split_2(value):
    high = lax.reduce_precision(value, 8, 7)
    return high.astype(jnp.bfloat16), (value - high).astype(jnp.bfloat16)


def local_hadamard(signed):
    rows, cols = signed.shape
    side = min(SIDE, rows)
    outer = rows // side
    table = jnp.asarray(hadamard_np(side), jnp.bfloat16)
    blocks = signed.reshape(outer, side, cols)
    high, low = split_2(blocks)
    dims = (((1,), (1,)), ((), ()))
    parts = []
    for index in range(outer):
        value = lax.dot_general(table, high[index], (((1,), (0,)), ((), ())), preferred_element_type=jnp.float32)
        value += lax.dot_general(table, low[index], (((1,), (0,)), ((), ())), preferred_element_type=jnp.float32)
        parts.append(value)
    step = 1
    while step < outer:
        nxt = list(parts)
        for index in range(outer):
            if not index & step:
                nxt[index] = parts[index] + parts[index | step]
                nxt[index | step] = parts[index] - parts[index | step]
        parts = nxt
        step *= 2
    return jnp.concatenate(parts, axis=0)


def body(spectrum, sign_bits, kept_rows, mask, w_init, h_init):
    damping = 1.0
    high = lax.Precision.HIGH
    block_count = lax.axis_size("frames")
    position = lax.axis_index("frames")
    frame_rows, cols = spectrum.shape
    per_block = kept_rows.shape[0] // block_count
    signed = spectrum * (1 - 2 * sign_bits).astype(jnp.float32)[:, None]
    local = local_hadamard(signed)
    value = jnp.take(local, kept_rows, axis=0, mode="clip").reshape(block_count, per_block, cols)
    levels = block_count.bit_length() - 1
    for level in range(levels):
        bit = jnp.bitwise_and(jnp.right_shift(position, level), 1)
        pairs = value.reshape(value.shape[0] // 2, 2, per_block, cols)
        keep = lax.dynamic_index_in_dim(pairs, bit, 1, keepdims=False)
        send = lax.dynamic_index_in_dim(pairs, 1 - bit, 1, keepdims=False)
        size = lax.axis_size("frames")
        got = lax.ppermute(send, "frames", [(i, i ^ 1 << level) for i in range(size)])
        value = jnp.where(bit == 1, got - keep, keep + got)
    sketch = value.reshape(per_block, cols)
    sketch = sketch / jnp.sqrt(jnp.float32(frame_rows * block_count))
    templates = h_init * mask.astype(jnp.float32)
    activations = w_init
    for round_index in range(ITERS):
        gram_h, proj = lax.psum(
            (
                jnp.dot(templates, templates.T, precision=high),
                jnp.dot(sketch, templates.T, precision=high),
            ),
            "bins",
        )
        lower = jnp.maximum(-proj, 0.0) + jnp.dot(activations, gram_h, precision=high) + damping
        activations = activations * jnp.sqrt((jnp.maximum(proj, 0.0) + damping) / lower)
        cross, gram_w = lax.psum(
            (
                jnp.dot(activations.T, sketch, precision=high),
                jnp.dot(activations.T, activations, precision=high),
            ),
            "frames",
        )
        lower = jnp.maximum(-cross, 0.0) + jnp.dot(gram_w, templates, precision=high) + damping
        templates = templates * jnp.sqrt((jnp.maximum(cross, 0.0) + damping) / lower)
    return (activations, templates)


MESH = pl.DeviceIdType.MESH
VMEM = pl.BlockSpec(memory_space=pltpu.VMEM)
DMA = pltpu.SemaphoreType.DMA
LIMIT = 48 * 1024 * 1024


def flip(index, mask):
    weight = 1
    result = index
    while weight <= mask:
        if mask & weight:
            result = result + weight - 2 * weight * lax.rem(index // weight, 2)
        weight *= 2
    return result


def greet(devices):
    barrier = pltpu.get_barrier_semaphore()
    for device in devices:
        pl.semaphore_signal(barrier, inc=1, device_id=device, device_id_type=MESH)
    pl.semaphore_wait(barrier, len(devices))


def send(src, dst, send_sem, recv_sem, device):
    copy = pltpu.make_async_remote_copy(
        src_ref=src, dst_ref=dst, send_sem=send_sem, recv_sem=recv_sem, device_id=device, device_id_type=MESH
    )
    copy.start()
    return copy


def piece(ref, index, size, base=0):
    return ref.at[pl.ds(pl.multiple_of(base + index * size, 8), size)]


def fold(bits, width):
    while width > 1:
        width //= 2
        bits = jnp.bitwise_xor(bits, jnp.right_shift(bits, width))
    return jnp.bitwise_and(bits, 1)


def sketch_kernel(
    scale, x_ref, s_ref, k_ref, g_ref, out_ref, g_out,
    term, high, low, rows_ref, got_y, got_z, part, g_core, g_sum, g_chip, send_sem, recv_sem,
):
    me, col = lax.axis_index("frames"), lax.axis_index("bins")
    core = lax.rem(col, 2)
    side = (flip(me, 1), col)
    near = (flip(me, 2), col)
    far = (flip(me, 4), col)
    sibling = (me, flip(col, 1))
    across = (me, flip(col, 2))
    greet([side, near, far, sibling, across])
    half = g_ref.shape[0] // 2
    gram_1 = send(piece(g_ref, 1 - core, half), g_core, send_sem.at[7], recv_sem.at[7], sibling)
    frame_rows = x_ref.shape[0]
    outer = frame_rows // SIDE
    tile = 128
    value = x_ref[...]
    rounded = value.astype(jnp.bfloat16)
    high[...] = rounded
    low[...] = (value - rounded.astype(jnp.float32)).astype(jnp.bfloat16)

    def compute(r):
        odd = 0
        for bit in range(3):
            if not r >> bit & 1:
                odd = odd + lax.rem(me // (1 << bit), 2)

        def step(index, carry):
            where = pl.ds(pl.multiple_of(index * tile, tile), tile)
            kept = k_ref[where, r : r + 1]
            lane = lax.broadcasted_iota(jnp.int32, (tile, SIDE), 1)
            bits = fold(jnp.bitwise_and(kept, lane), SIDE.bit_length() - 1)
            table = (1 - 2 * jnp.bitwise_and(bits + odd, 1)).astype(jnp.float32)
            upper = jnp.right_shift(kept, 8)
            for a in range(outer):
                sign = (1 - 2 * fold(jnp.bitwise_and(upper, a), 8)).astype(jnp.float32)
                cols = slice(a * SIDE, (a + 1) * SIDE)
                flips = (1 - 2 * s_ref[:, cols]).astype(jnp.float32)
                rows_ref[:, cols] = ((table * sign) * flips).astype(jnp.bfloat16)
            rows = rows_ref[...]
            term[r, where] = jnp.dot(rows, high[...], preferred_element_type=jnp.float32) + jnp.dot(
                rows, low[...], preferred_element_type=jnp.float32
            )
            return carry

        lax.fori_loop(0, k_ref.shape[0] // tile, step, 0)

    copies = {}
    for z in (3, 2, 1, 0):
        compute(2 * z + 1)
        copies[z] = send(term.at[2 * z + 1], got_y.at[z], send_sem.at[z], recv_sem.at[z], side)
        if z == 3:
            gram_1.wait_recv()
            g_sum[...] = piece(g_ref, core, half)[...] + g_core[...]
            gram_2 = send(g_sum, g_chip, send_sem.at[8], recv_sem.at[8], across)
    compute(6)
    copies[3].wait_recv()
    part[0] = term[6] + got_y[3]
    first = send(part.at[0], got_z.at[0], send_sem.at[4], recv_sem.at[4], near)
    compute(4)
    gram_2.wait_recv()
    mine = piece(g_out, core, half)
    mine[...] = g_sum[...] + g_chip[...]
    gram_3 = send(mine, mine, send_sem.at[9], recv_sem.at[9], sibling)
    compute(2)
    copies[2].wait_recv()
    first.wait_recv()
    part[1] = term[4] + got_y[2] + got_z[0]
    second = send(part.at[1], got_z.at[1], send_sem.at[5], recv_sem.at[5], far)
    compute(0)
    copies[1].wait_recv()
    part[2] = term[2] + got_y[1]
    third = send(part.at[2], got_z.at[2], send_sem.at[6], recv_sem.at[6], near)
    copies[0].wait_recv()
    third.wait_recv()
    second.wait_recv()
    out_ref[...] = ((term[0] + got_y[0]) + (got_z[2] + got_z[1])) * scale
    gram_3.wait_recv()
    for copy in (*copies.values(), first, second, third, gram_1, gram_2, gram_3):
        copy.wait_send()


def make_sketch(spectrum, sign_row, kept, gram, scale):
    frame_rows, cols = spectrum.shape
    rows = kept.shape[0]
    half = (gram.shape[0] // 2, gram.shape[1])
    f32, bf16 = jnp.float32, jnp.bfloat16
    return pl.pallas_call(
        lambda *refs: sketch_kernel(scale, *refs),
        out_shape=(jax.ShapeDtypeStruct((rows, cols), f32), jax.ShapeDtypeStruct(gram.shape, f32)),
        in_specs=[VMEM] * 4,
        out_specs=(VMEM, VMEM),
        scratch_shapes=[
            pltpu.VMEM((8, rows, cols), f32),
            pltpu.VMEM((frame_rows, cols), bf16),
            pltpu.VMEM((frame_rows, cols), bf16),
            pltpu.VMEM((128, frame_rows), bf16),
            pltpu.VMEM((4, rows, cols), f32),
            pltpu.VMEM((3, rows, cols), f32),
            pltpu.VMEM((3, rows, cols), f32),
            pltpu.VMEM(half, f32),
            pltpu.VMEM(half, f32),
            pltpu.VMEM(half, f32),
            DMA((10,)),
            DMA((10,)),
        ],
        compiler_params=pltpu.CompilerParams(collective_id=0, has_side_effects=True, vmem_limit_bytes=LIMIT),
        name="make_sketch",
    )(spectrum, sign_row, kept, gram)


def bins_kernel(count, *refs):
    ins, outs = refs[:count], refs[count : 2 * count]
    from_core, sums, from_chip = (refs[(2 + i) * count : (3 + i) * count] for i in range(3))
    send_sem, recv_sem = refs[5 * count :]
    row, me = lax.axis_index("frames"), lax.axis_index("bins")
    core = lax.rem(me, 2)
    sibling = (row, flip(me, 1))
    across = (row, flip(me, 2))
    greet([sibling, across])
    cuts = []
    for k in range(count):
        half = ins[k].shape[0] // 2
        size = half // 2
        for part in range(2):
            cuts.append((k, half, part * size, size))
    stage_1, stage_2, stage_3 = [], [], []
    for n, (k, half, start, size) in enumerate(cuts):
        theirs = ins[k].at[pl.ds(pl.multiple_of((1 - core) * half + start, 8), size)]
        got = from_core[k].at[pl.ds(start, size)]
        stage_1.append(send(theirs, got, send_sem.at[n], recv_sem.at[n], sibling))
    for n, (k, half, start, size) in enumerate(cuts):
        stage_1[n].wait_recv()
        here = pl.ds(start, size)
        sums[k][here] = ins[k][pl.ds(pl.multiple_of(core * half + start, 8), size)] + from_core[k][here]
        stage_2.append(send(sums[k].at[here], from_chip[k].at[here], send_sem.at[8 + n], recv_sem.at[8 + n], across))
    for n, (k, half, start, size) in enumerate(cuts):
        stage_2[n].wait_recv()
        here = pl.ds(start, size)
        mine = outs[k].at[pl.ds(pl.multiple_of(core * half + start, 8), size)]
        mine[...] = sums[k][here] + from_chip[k][here]
        stage_3.append(send(mine, mine, send_sem.at[16 + n], recv_sem.at[16 + n], sibling))
    for copy in stage_3:
        copy.wait_recv()
    for copy in (*stage_1, *stage_2, *stage_3):
        copy.wait_send()


def sum_bins(name, collective_id, *arrays):
    f32 = jnp.float32
    count = len(arrays)
    halves = [(array.shape[0] // 2, array.shape[1]) for array in arrays]
    return pl.pallas_call(
        lambda *refs: bins_kernel(count, *refs),
        out_shape=tuple(jax.ShapeDtypeStruct(array.shape, f32) for array in arrays),
        in_specs=[VMEM] * count,
        out_specs=(VMEM,) * count,
        scratch_shapes=[pltpu.VMEM(shape, f32) for _ in range(3) for shape in halves] + [DMA((24,)), DMA((24,))],
        compiler_params=pltpu.CompilerParams(collective_id=collective_id, has_side_effects=True, vmem_limit_bytes=LIMIT),
        name=name,
    )(*arrays)


def frames_kernel(g_ref, c_ref, g_out, c_out, g_y, c_y, g_z, c_z, g_part, c_part, send_sem, recv_sem):
    me, col = lax.axis_index("frames"), lax.axis_index("bins")
    core = lax.rem(col, 2)
    side = (flip(me, 1), col)
    peers = {z: (flip(me, 2 * z), col) for z in (3, 2, 1)}
    sibling = (me, flip(col, 1))
    greet([side, *peers.values(), sibling])
    g_half = g_ref.shape[0]
    arrays = (
        (0, g_ref, g_half // 8, g_y, g_z, g_part, g_out, core * g_half),
        (16, c_ref, c_ref.shape[0] // 8, c_y, c_z, c_part, c_out, 0),
    )
    copies = []

    def go(src, dst, n, device):
        copies.append(send(src, dst, send_sem.at[n], recv_sem.at[n], device))
        return copies[-1]

    by_y, by_z, back, passed = {}, {}, {}, {}
    for k, src, size, from_y, from_z, part, out, base in arrays:
        for z in (3, 2, 1, 0):
            by_y[k, z] = go(piece(src, flip(me, 2 * z + 1), size), from_y.at[z], k + z, side)
    for k, src, size, from_y, from_z, part, out, base in arrays:
        for z in (3, 2, 1):
            by_y[k, z].wait_recv()
            part[z - 1] = piece(src, flip(me, 2 * z), size)[...] + from_y[z]
            by_z[k, z] = go(part.at[z - 1], from_z.at[z - 1], k + 4 + z, peers[z])
    for k, src, size, from_y, from_z, part, out, base in arrays:
        by_y[k, 0].wait_recv()
        total = piece(src, me, size)[...] + from_y[0]
        for z in (1, 2, 3):
            by_z[k, z].wait_recv()
            total = total + from_z[z - 1]
        mine = piece(out, me, size, base)
        mine[...] = total
        for z in (3, 2, 1):
            back[k, z] = go(mine, mine, k + 8 + z, peers[z])
        back[k, 0] = go(mine, mine, k + 8, side)
    for k, src, size, from_y, from_z, part, out, base in arrays:
        for z in (1, 2, 3):
            back[k, z].wait_recv()
            theirs = piece(out, flip(me, 2 * z), size, base)
            passed[k, z] = go(theirs, theirs, k + 12 + z, side)
        if k == 0:
            back[k, 0].wait_recv()
            for z in (1, 2, 3):
                passed[k, z].wait_recv()
            mine = piece(g_out, core, g_half)
            swap = go(mine, mine, 12, sibling)
    back[16, 0].wait_recv()
    for z in (1, 2, 3):
        passed[16, z].wait_recv()
    swap.wait_recv()
    for copy in copies:
        copy.wait_send()


def sum_frames(gram_half, cross):
    f32 = jnp.float32
    parts, cols = cross.shape
    g_piece = (gram_half.shape[0] // 8, gram_half.shape[1])
    c_piece = (parts // 8, cols)
    return pl.pallas_call(
        frames_kernel,
        out_shape=(
            jax.ShapeDtypeStruct((2 * gram_half.shape[0], gram_half.shape[1]), f32),
            jax.ShapeDtypeStruct(cross.shape, f32),
        ),
        in_specs=[VMEM, VMEM],
        out_specs=(VMEM, VMEM),
        scratch_shapes=[pltpu.VMEM((count, *shape), f32) for count in (4, 3, 3) for shape in (g_piece, c_piece)]
        + [DMA((32,)), DMA((32,))],
        compiler_params=pltpu.CompilerParams(collective_id=2, has_side_effects=True, vmem_limit_bytes=LIMIT),
        name="sum_frames",
    )(gram_half, cross)


def body_8x4(spectrum, sign_bits, kept_rows, mask, w_init, h_init):
    damping = 1.0
    high = lax.Precision.HIGH
    block_count = 8
    position = lax.axis_index("frames")
    core = lax.rem(lax.axis_index("bins"), 2)
    frame_rows, cols = spectrum.shape
    per_block = kept_rows.shape[0] // block_count
    parts = w_init.shape[1]
    padded = -(-parts // 128) * 128
    templates = jnp.pad(h_init * mask.astype(jnp.float32), ((0, padded - parts), (0, 0)))
    activations = jnp.pad(w_init, ((0, 0), (0, padded - parts)))
    blocks = jnp.bitwise_xor(position, jnp.arange(block_count, dtype=jnp.int32))
    kept = jnp.take(kept_rows.reshape(block_count, per_block), blocks, axis=0, mode="clip").T
    sketch, gram_h = make_sketch(
        spectrum,
        sign_bits.reshape(1, frame_rows),
        kept,
        jnp.dot(templates, templates.T, precision=high),
        1.0 / (frame_rows * block_count) ** 0.5,
    )
    half = padded // 2
    for round_index in range(ITERS):
        proj = jnp.dot(sketch, templates.T, precision=high)
        if round_index == 0:
            (proj,) = sum_bins("sum_proj", 1, proj)
        else:
            gram_h, proj = sum_bins("sum_both", 3, jnp.dot(templates, templates.T, precision=high), proj)
        lower = jnp.maximum(-proj, 0.0) + jnp.dot(activations, gram_h, precision=high) + damping
        activations = activations * jnp.sqrt((jnp.maximum(proj, 0.0) + damping) / lower)
        own = lax.dynamic_slice_in_dim(activations, core * half, half, axis=1)
        gram_w, cross = sum_frames(
            jnp.dot(own.T, activations, precision=high),
            jnp.dot(activations.T, sketch, precision=high),
        )
        lower = jnp.maximum(-cross, 0.0) + jnp.dot(gram_w, templates, precision=high) + damping
        templates = templates * jnp.sqrt((jnp.maximum(cross, 0.0) + damping) / lower)
    return (activations[:, :parts], templates[:parts])


def solution(mesh):
    in_specs = (
        P("frames", "bins"),
        P("frames"),
        P(),
        P(None, "bins"),
        P("frames", None),
        P(None, "bins"),
    )
    out_specs = (P("frames", None), P(None, "bins"))
    small = mesh.shape["frames"] == 8 and mesh.shape["bins"] == 4
    return jax.shard_map(body_8x4 if small else body, mesh=mesh, in_specs=in_specs, out_specs=out_specs, check_vma=False)
```

```python
import jax
import jax.numpy as jnp
import numpy as np
from jax import lax
from jax.experimental import pallas as pl
from jax.experimental.pallas import tpu as pltpu
from jax.sharding import PartitionSpec as P

ITERS = 2
SIDE = 256


def hadamard_np(count):
    table = np.ones((1, 1), np.float32)
    while table.shape[0] < count:
        table = np.block([[table, table], [table, -table]])
    return table


def split_2(value):
    high = lax.reduce_precision(value, 8, 7)
    return high.astype(jnp.bfloat16), (value - high).astype(jnp.bfloat16)


def local_hadamard(signed):
    rows, cols = signed.shape
    side = min(SIDE, rows)
    outer = rows // side
    table = jnp.asarray(hadamard_np(side), jnp.bfloat16)
    blocks = signed.reshape(outer, side, cols)
    high, low = split_2(blocks)
    dims = (((1,), (1,)), ((), ()))
    parts = []
    for index in range(outer):
        value = lax.dot_general(table, high[index], (((1,), (0,)), ((), ())), preferred_element_type=jnp.float32)
        value += lax.dot_general(table, low[index], (((1,), (0,)), ((), ())), preferred_element_type=jnp.float32)
        parts.append(value)
    step = 1
    while step < outer:
        nxt = list(parts)
        for index in range(outer):
            if not index & step:
                nxt[index] = parts[index] + parts[index | step]
                nxt[index | step] = parts[index] - parts[index | step]
        parts = nxt
        step *= 2
    return jnp.concatenate(parts, axis=0)


def body(spectrum, sign_bits, kept_rows, mask, w_init, h_init):
    damping = 1.0
    high = lax.Precision.HIGH
    block_count = lax.axis_size("frames")
    position = lax.axis_index("frames")
    frame_rows, cols = spectrum.shape
    per_block = kept_rows.shape[0] // block_count
    signed = spectrum * (1 - 2 * sign_bits).astype(jnp.float32)[:, None]
    local = local_hadamard(signed)
    value = jnp.take(local, kept_rows, axis=0, mode="clip").reshape(block_count, per_block, cols)
    levels = block_count.bit_length() - 1
    for level in range(levels):
        bit = jnp.bitwise_and(jnp.right_shift(position, level), 1)
        pairs = value.reshape(value.shape[0] // 2, 2, per_block, cols)
        keep = lax.dynamic_index_in_dim(pairs, bit, 1, keepdims=False)
        send = lax.dynamic_index_in_dim(pairs, 1 - bit, 1, keepdims=False)
        size = lax.axis_size("frames")
        got = lax.ppermute(send, "frames", [(i, i ^ 1 << level) for i in range(size)])
        value = jnp.where(bit == 1, got - keep, keep + got)
    sketch = value.reshape(per_block, cols)
    sketch = sketch / jnp.sqrt(jnp.float32(frame_rows * block_count))
    templates = h_init * mask.astype(jnp.float32)
    activations = w_init
    for round_index in range(ITERS):
        gram_h, proj = lax.psum(
            (
                jnp.dot(templates, templates.T, precision=high),
                jnp.dot(sketch, templates.T, precision=high),
            ),
            "bins",
        )
        lower = jnp.maximum(-proj, 0.0) + jnp.dot(activations, gram_h, precision=high) + damping
        activations = activations * jnp.sqrt((jnp.maximum(proj, 0.0) + damping) / lower)
        cross, gram_w = lax.psum(
            (
                jnp.dot(activations.T, sketch, precision=high),
                jnp.dot(activations.T, activations, precision=high),
            ),
            "frames",
        )
        lower = jnp.maximum(-cross, 0.0) + jnp.dot(gram_w, templates, precision=high) + damping
        templates = templates * jnp.sqrt((jnp.maximum(cross, 0.0) + damping) / lower)
    return (activations, templates)


MESH = pl.DeviceIdType.MESH
VMEM = pl.BlockSpec(memory_space=pltpu.VMEM)
DMA = pltpu.SemaphoreType.DMA
LIMIT = 48 * 1024 * 1024


def flip(index, mask):
    weight = 1
    result = index
    while weight <= mask:
        if mask & weight:
            result = result + weight - 2 * weight * lax.rem(index // weight, 2)
        weight *= 2
    return result


def greet(devices):
    barrier = pltpu.get_barrier_semaphore()
    for device in devices:
        pl.semaphore_signal(barrier, inc=1, device_id=device, device_id_type=MESH)
    pl.semaphore_wait(barrier, len(devices))


def send(src, dst, send_sem, recv_sem, device):
    copy = pltpu.make_async_remote_copy(
        src_ref=src, dst_ref=dst, send_sem=send_sem, recv_sem=recv_sem, device_id=device, device_id_type=MESH
    )
    copy.start()
    return copy


def piece(ref, index, size, base=0):
    return ref.at[pl.ds(pl.multiple_of(base + index * size, 8), size)]


def fold(bits, width):
    while width > 1:
        width //= 2
        bits = jnp.bitwise_xor(bits, jnp.right_shift(bits, width))
    return jnp.bitwise_and(bits, 1)


def sketch_kernel(
    scale, x_ref, s_ref, k_ref, g_ref, t_ref, out_ref, g_out, p_out,
    term, high, low, rows_ref, got_y, got_z, part, g_core, g_sum, g_chip,
    proj, p_core, p_sum, p_chip, send_sem, recv_sem,
):
    me, col = lax.axis_index("frames"), lax.axis_index("bins")
    core = lax.rem(col, 2)
    side = (flip(me, 1), col)
    near = (flip(me, 2), col)
    far = (flip(me, 4), col)
    sibling = (me, flip(col, 1))
    across = (me, flip(col, 2))
    greet([side, near, far, sibling, across])
    half = g_ref.shape[0] // 2
    gram_1 = send(piece(g_ref, 1 - core, half), g_core, send_sem.at[14], recv_sem.at[14], sibling)
    frame_rows = x_ref.shape[0]
    outer = frame_rows // SIDE
    tile = 128
    span = k_ref.shape[0] // 2
    share = span // 2
    spans = [pl.ds(0, span), pl.ds(span, span)]
    value = x_ref[...]
    rounded = value.astype(jnp.bfloat16)
    high[...] = rounded
    low[...] = (value - rounded.astype(jnp.float32)).astype(jnp.bfloat16)

    def compute(r, h):
        odd = 0
        for bit in range(3):
            if not r >> bit & 1:
                odd = odd + lax.rem(me // (1 << bit), 2)

        def step(index, carry):
            where = pl.ds(pl.multiple_of(h * span + index * tile, tile), tile)
            kept = k_ref[where, r : r + 1]
            lane = lax.broadcasted_iota(jnp.int32, (tile, SIDE), 1)
            bits = fold(jnp.bitwise_and(kept, lane), SIDE.bit_length() - 1)
            table = (1 - 2 * jnp.bitwise_and(bits + odd, 1)).astype(jnp.float32)
            upper = jnp.right_shift(kept, 8)
            for a in range(outer):
                sign = (1 - 2 * fold(jnp.bitwise_and(upper, a), 8)).astype(jnp.float32)
                cols = slice(a * SIDE, (a + 1) * SIDE)
                flips = (1 - 2 * s_ref[:, cols]).astype(jnp.float32)
                rows_ref[:, cols] = ((table * sign) * flips).astype(jnp.bfloat16)
            rows = rows_ref[...]
            term[r, where] = jnp.dot(rows, high[...], preferred_element_type=jnp.float32) + jnp.dot(
                rows, low[...], preferred_element_type=jnp.float32
            )
            return carry

        lax.fori_loop(0, span // tile, step, 0)

    copies = []

    def go(src, dst, n, device):
        copies.append(send(src, dst, send_sem.at[n], recv_sem.at[n], device))
        return copies[-1]

    by_y, first, second, third, proj_1, proj_2, proj_3 = ({} for _ in range(7))

    def odd_terms(h):
        for z in (3, 2, 1, 0):
            compute(2 * z + 1, h)
            by_y[h, z] = go(term.at[2 * z + 1, spans[h]], got_y.at[z, spans[h]], 4 * h + z, side)

    def to_near(h):
        by_y[h, 3].wait_recv()
        part[0, spans[h]] = term[6, spans[h]] + got_y[3, spans[h]]
        first[h] = go(part.at[0, spans[h]], got_z.at[0, spans[h]], 8 + 3 * h, near)

    def to_far(h):
        by_y[h, 2].wait_recv()
        first[h].wait_recv()
        part[1, spans[h]] = term[4, spans[h]] + got_y[2, spans[h]] + got_z[0, spans[h]]
        second[h] = go(part.at[1, spans[h]], got_z.at[1, spans[h]], 9 + 3 * h, far)

    def last_near(h):
        by_y[h, 1].wait_recv()
        part[2, spans[h]] = term[2, spans[h]] + got_y[1, spans[h]]
        third[h] = go(part.at[2, spans[h]], got_z.at[2, spans[h]], 10 + 3 * h, near)

    def split(value):
        top = value.astype(jnp.bfloat16)
        return top, (value - top.astype(jnp.float32)).astype(jnp.bfloat16)

    def finish(h):
        here = spans[h]
        by_y[h, 0].wait_recv()
        third[h].wait_recv()
        second[h].wait_recv()
        sketch = ((term[0, here] + got_y[0, here]) + (got_z[2, here] + got_z[1, here])) * scale
        out_ref[here] = sketch
        s_high, s_low = split(sketch)
        t_high, t_low = split(t_ref[...])

        def dot(left, right):
            return lax.dot_general(left, right, (((1,), (1,)), ((), ())), preferred_element_type=jnp.float32)

        proj[here] = dot(s_high, t_high) + (dot(s_high, t_low) + dot(s_low, t_high))
        theirs = piece(proj, 1 - core, share, h * span)
        proj_1[h] = go(theirs, p_core.at[h], 17 + 3 * h, sibling)

    def proj_across(h):
        proj_1[h].wait_recv()
        p_sum[h] = piece(proj, core, share, h * span)[...] + p_core[h]
        proj_2[h] = go(p_sum.at[h], p_chip.at[h], 18 + 3 * h, across)

    def proj_back(h):
        proj_2[h].wait_recv()
        mine = piece(p_out, core, share, h * span)
        mine[...] = p_sum[h] + p_chip[h]
        proj_3[h] = go(mine, mine, 19 + 3 * h, sibling)

    odd_terms(0)
    gram_1.wait_recv()
    g_sum[...] = piece(g_ref, core, half)[...] + g_core[...]
    gram_2 = go(g_sum, g_chip, 15, across)
    compute(6, 0)
    to_near(0)
    compute(4, 0)
    odd_terms(1)
    to_far(0)
    compute(2, 0)
    compute(0, 0)
    last_near(0)
    gram_2.wait_recv()
    mine = piece(g_out, core, half)
    mine[...] = g_sum[...] + g_chip[...]
    gram_3 = go(mine, mine, 16, sibling)
    for r in (6, 4, 2, 0):
        compute(r, 1)
    finish(0)
    to_near(1)
    proj_across(0)
    to_far(1)
    proj_back(0)
    last_near(1)
    finish(1)
    proj_across(1)
    proj_back(1)
    gram_3.wait_recv()
    for h in (0, 1):
        proj_3[h].wait_recv()
    for copy in (gram_1, *copies):
        copy.wait_send()


def make_sketch(spectrum, sign_row, kept, gram, templates, scale):
    frame_rows, cols = spectrum.shape
    rows = kept.shape[0]
    parts = templates.shape[0]
    half = (gram.shape[0] // 2, gram.shape[1])
    f32, bf16 = jnp.float32, jnp.bfloat16
    return pl.pallas_call(
        lambda *refs: sketch_kernel(scale, *refs),
        out_shape=(jax.ShapeDtypeStruct((rows, cols), f32), jax.ShapeDtypeStruct(gram.shape, f32), jax.ShapeDtypeStruct((rows, parts), f32)),
        in_specs=[VMEM] * 5,
        out_specs=(VMEM, VMEM, VMEM),
        scratch_shapes=[
            pltpu.VMEM((8, rows, cols), f32),
            pltpu.VMEM((frame_rows, cols), bf16),
            pltpu.VMEM((frame_rows, cols), bf16),
            pltpu.VMEM((128, frame_rows), bf16),
            pltpu.VMEM((4, rows, cols), f32),
            pltpu.VMEM((3, rows, cols), f32),
            pltpu.VMEM((3, rows, cols), f32),
            pltpu.VMEM(half, f32),
            pltpu.VMEM(half, f32),
            pltpu.VMEM(half, f32),
            pltpu.VMEM((rows, parts), f32),
            pltpu.VMEM((2, rows // 4, parts), f32),
            pltpu.VMEM((2, rows // 4, parts), f32),
            pltpu.VMEM((2, rows // 4, parts), f32),
            DMA((23,)),
            DMA((23,)),
        ],
        compiler_params=pltpu.CompilerParams(collective_id=0, has_side_effects=True, vmem_limit_bytes=LIMIT),
        name="make_sketch",
    )(spectrum, sign_row, kept, gram, templates)


def bins_kernel(count, *refs):
    ins, outs = refs[:count], refs[count : 2 * count]
    from_core, sums, from_chip = (refs[(2 + i) * count : (3 + i) * count] for i in range(3))
    send_sem, recv_sem = refs[5 * count :]
    row, me = lax.axis_index("frames"), lax.axis_index("bins")
    core = lax.rem(me, 2)
    sibling = (row, flip(me, 1))
    across = (row, flip(me, 2))
    greet([sibling, across])
    cuts = []
    for k in range(count):
        half = ins[k].shape[0] // 2
        size = half // 2
        for part in range(2):
            cuts.append((k, half, part * size, size))
    stage_1, stage_2, stage_3 = [], [], []
    for n, (k, half, start, size) in enumerate(cuts):
        theirs = ins[k].at[pl.ds(pl.multiple_of((1 - core) * half + start, 8), size)]
        got = from_core[k].at[pl.ds(start, size)]
        stage_1.append(send(theirs, got, send_sem.at[n], recv_sem.at[n], sibling))
    for n, (k, half, start, size) in enumerate(cuts):
        stage_1[n].wait_recv()
        here = pl.ds(start, size)
        sums[k][here] = ins[k][pl.ds(pl.multiple_of(core * half + start, 8), size)] + from_core[k][here]
        stage_2.append(send(sums[k].at[here], from_chip[k].at[here], send_sem.at[8 + n], recv_sem.at[8 + n], across))
    for n, (k, half, start, size) in enumerate(cuts):
        stage_2[n].wait_recv()
        here = pl.ds(start, size)
        mine = outs[k].at[pl.ds(pl.multiple_of(core * half + start, 8), size)]
        mine[...] = sums[k][here] + from_chip[k][here]
        stage_3.append(send(mine, mine, send_sem.at[16 + n], recv_sem.at[16 + n], sibling))
    for copy in stage_3:
        copy.wait_recv()
    for copy in (*stage_1, *stage_2, *stage_3):
        copy.wait_send()


def sum_bins(name, collective_id, *arrays):
    f32 = jnp.float32
    count = len(arrays)
    halves = [(array.shape[0] // 2, array.shape[1]) for array in arrays]
    return pl.pallas_call(
        lambda *refs: bins_kernel(count, *refs),
        out_shape=tuple(jax.ShapeDtypeStruct(array.shape, f32) for array in arrays),
        in_specs=[VMEM] * count,
        out_specs=(VMEM,) * count,
        scratch_shapes=[pltpu.VMEM(shape, f32) for _ in range(3) for shape in halves] + [DMA((24,)), DMA((24,))],
        compiler_params=pltpu.CompilerParams(collective_id=collective_id, has_side_effects=True, vmem_limit_bytes=LIMIT),
        name=name,
    )(*arrays)


def frames_kernel(g_ref, c_ref, g_out, c_out, g_y, c_y, g_z, c_z, g_part, c_part, send_sem, recv_sem):
    me, col = lax.axis_index("frames"), lax.axis_index("bins")
    core = lax.rem(col, 2)
    side = (flip(me, 1), col)
    peers = {z: (flip(me, 2 * z), col) for z in (3, 2, 1)}
    sibling = (me, flip(col, 1))
    greet([side, *peers.values(), sibling])
    g_half = g_ref.shape[0]
    arrays = (
        (0, g_ref, g_half // 8, g_y, g_z, g_part, g_out, core * g_half),
        (16, c_ref, c_ref.shape[0] // 8, c_y, c_z, c_part, c_out, 0),
    )
    copies = []

    def go(src, dst, n, device):
        copies.append(send(src, dst, send_sem.at[n], recv_sem.at[n], device))
        return copies[-1]

    by_y, by_z, back, passed = {}, {}, {}, {}
    for k, src, size, from_y, from_z, part, out, base in arrays:
        for z in (3, 2, 1, 0):
            by_y[k, z] = go(piece(src, flip(me, 2 * z + 1), size), from_y.at[z], k + z, side)
    for k, src, size, from_y, from_z, part, out, base in arrays:
        for z in (3, 2, 1):
            by_y[k, z].wait_recv()
            part[z - 1] = piece(src, flip(me, 2 * z), size)[...] + from_y[z]
            by_z[k, z] = go(part.at[z - 1], from_z.at[z - 1], k + 4 + z, peers[z])
    for k, src, size, from_y, from_z, part, out, base in arrays:
        by_y[k, 0].wait_recv()
        total = piece(src, me, size)[...] + from_y[0]
        for z in (1, 2, 3):
            by_z[k, z].wait_recv()
            total = total + from_z[z - 1]
        mine = piece(out, me, size, base)
        mine[...] = total
        for z in (3, 2, 1):
            back[k, z] = go(mine, mine, k + 8 + z, peers[z])
        back[k, 0] = go(mine, mine, k + 8, side)
    for k, src, size, from_y, from_z, part, out, base in arrays:
        for z in (1, 2, 3):
            back[k, z].wait_recv()
            theirs = piece(out, flip(me, 2 * z), size, base)
            passed[k, z] = go(theirs, theirs, k + 12 + z, side)
        if k == 0:
            back[k, 0].wait_recv()
            for z in (1, 2, 3):
                passed[k, z].wait_recv()
            mine = piece(g_out, core, g_half)
            swap = go(mine, mine, 12, sibling)
    back[16, 0].wait_recv()
    for z in (1, 2, 3):
        passed[16, z].wait_recv()
    swap.wait_recv()
    for copy in copies:
        copy.wait_send()


def sum_frames(gram_half, cross):
    f32 = jnp.float32
    parts, cols = cross.shape
    g_piece = (gram_half.shape[0] // 8, gram_half.shape[1])
    c_piece = (parts // 8, cols)
    return pl.pallas_call(
        frames_kernel,
        out_shape=(
            jax.ShapeDtypeStruct((2 * gram_half.shape[0], gram_half.shape[1]), f32),
            jax.ShapeDtypeStruct(cross.shape, f32),
        ),
        in_specs=[VMEM, VMEM],
        out_specs=(VMEM, VMEM),
        scratch_shapes=[pltpu.VMEM((count, *shape), f32) for count in (4, 3, 3) for shape in (g_piece, c_piece)]
        + [DMA((32,)), DMA((32,))],
        compiler_params=pltpu.CompilerParams(collective_id=2, has_side_effects=True, vmem_limit_bytes=LIMIT),
        name="sum_frames",
    )(gram_half, cross)


def body_8x4(spectrum, sign_bits, kept_rows, mask, w_init, h_init):
    damping = 1.0
    high = lax.Precision.HIGH
    block_count = 8
    position = lax.axis_index("frames")
    core = lax.rem(lax.axis_index("bins"), 2)
    frame_rows, cols = spectrum.shape
    per_block = kept_rows.shape[0] // block_count
    parts = w_init.shape[1]
    padded = -(-parts // 128) * 128
    templates = jnp.pad(h_init * mask.astype(jnp.float32), ((0, padded - parts), (0, 0)))
    activations = jnp.pad(w_init, ((0, 0), (0, padded - parts)))
    blocks = jnp.bitwise_xor(position, jnp.arange(block_count, dtype=jnp.int32))
    kept = jnp.take(kept_rows.reshape(block_count, per_block), blocks, axis=0, mode="clip").T
    sketch, gram_h, proj = make_sketch(
        spectrum,
        sign_bits.reshape(1, frame_rows),
        kept,
        jnp.dot(templates, templates.T, precision=high),
        templates,
        1.0 / (frame_rows * block_count) ** 0.5,
    )
    half = padded // 2
    for round_index in range(ITERS):
        if round_index:
            gram_h, proj = sum_bins(
                "sum_bins",
                1,
                jnp.dot(templates, templates.T, precision=high),
                jnp.dot(sketch, templates.T, precision=high),
            )
        lower = jnp.maximum(-proj, 0.0) + jnp.dot(activations, gram_h, precision=high) + damping
        activations = activations * jnp.sqrt((jnp.maximum(proj, 0.0) + damping) / lower)
        own = lax.dynamic_slice_in_dim(activations, core * half, half, axis=1)
        gram_w, cross = sum_frames(
            jnp.dot(own.T, activations, precision=high),
            jnp.dot(activations.T, sketch, precision=high),
        )
        lower = jnp.maximum(-cross, 0.0) + jnp.dot(gram_w, templates, precision=high) + damping
        templates = templates * jnp.sqrt((jnp.maximum(cross, 0.0) + damping) / lower)
    return (activations[:, :parts], templates[:parts])


def solution(mesh):
    in_specs = (
        P("frames", "bins"),
        P("frames"),
        P(),
        P(None, "bins"),
        P("frames", None),
        P(None, "bins"),
    )
    out_specs = (P("frames", None), P(None, "bins"))
    small = mesh.shape["frames"] == 8 and mesh.shape["bins"] == 4
    return jax.shard_map(body_8x4 if small else body, mesh=mesh, in_specs=in_specs, out_specs=out_specs, check_vma=False)
```

```python
import jax
import jax.numpy as jnp
import numpy as np
from jax import lax
from jax.experimental import pallas as pl
from jax.experimental.pallas import tpu as pltpu
from jax.sharding import PartitionSpec as P

ITERS = 2
SIDE = 256


def hadamard_np(count):
    table = np.ones((1, 1), np.float32)
    while table.shape[0] < count:
        table = np.block([[table, table], [table, -table]])
    return table


def split_2(value):
    high = lax.reduce_precision(value, 8, 7)
    return high.astype(jnp.bfloat16), (value - high).astype(jnp.bfloat16)


def local_hadamard(signed):
    rows, cols = signed.shape
    side = min(SIDE, rows)
    outer = rows // side
    table = jnp.asarray(hadamard_np(side), jnp.bfloat16)
    blocks = signed.reshape(outer, side, cols)
    high, low = split_2(blocks)
    dims = (((1,), (1,)), ((), ()))
    parts = []
    for index in range(outer):
        value = lax.dot_general(table, high[index], (((1,), (0,)), ((), ())), preferred_element_type=jnp.float32)
        value += lax.dot_general(table, low[index], (((1,), (0,)), ((), ())), preferred_element_type=jnp.float32)
        parts.append(value)
    step = 1
    while step < outer:
        nxt = list(parts)
        for index in range(outer):
            if not index & step:
                nxt[index] = parts[index] + parts[index | step]
                nxt[index | step] = parts[index] - parts[index | step]
        parts = nxt
        step *= 2
    return jnp.concatenate(parts, axis=0)


def body(spectrum, sign_bits, kept_rows, mask, w_init, h_init):
    damping = 1.0
    high = lax.Precision.HIGH
    block_count = lax.axis_size("frames")
    position = lax.axis_index("frames")
    frame_rows, cols = spectrum.shape
    per_block = kept_rows.shape[0] // block_count
    signed = spectrum * (1 - 2 * sign_bits).astype(jnp.float32)[:, None]
    local = local_hadamard(signed)
    value = jnp.take(local, kept_rows, axis=0, mode="clip").reshape(block_count, per_block, cols)
    levels = block_count.bit_length() - 1
    for level in range(levels):
        bit = jnp.bitwise_and(jnp.right_shift(position, level), 1)
        pairs = value.reshape(value.shape[0] // 2, 2, per_block, cols)
        keep = lax.dynamic_index_in_dim(pairs, bit, 1, keepdims=False)
        send = lax.dynamic_index_in_dim(pairs, 1 - bit, 1, keepdims=False)
        size = lax.axis_size("frames")
        got = lax.ppermute(send, "frames", [(i, i ^ 1 << level) for i in range(size)])
        value = jnp.where(bit == 1, got - keep, keep + got)
    sketch = value.reshape(per_block, cols)
    sketch = sketch / jnp.sqrt(jnp.float32(frame_rows * block_count))
    templates = h_init * mask.astype(jnp.float32)
    activations = w_init
    for round_index in range(ITERS):
        gram_h, proj = lax.psum(
            (
                jnp.dot(templates, templates.T, precision=high),
                jnp.dot(sketch, templates.T, precision=high),
            ),
            "bins",
        )
        lower = jnp.maximum(-proj, 0.0) + jnp.dot(activations, gram_h, precision=high) + damping
        activations = activations * jnp.sqrt((jnp.maximum(proj, 0.0) + damping) / lower)
        cross, gram_w = lax.psum(
            (
                jnp.dot(activations.T, sketch, precision=high),
                jnp.dot(activations.T, activations, precision=high),
            ),
            "frames",
        )
        lower = jnp.maximum(-cross, 0.0) + jnp.dot(gram_w, templates, precision=high) + damping
        templates = templates * jnp.sqrt((jnp.maximum(cross, 0.0) + damping) / lower)
    return (activations, templates)


MESH = pl.DeviceIdType.MESH
VMEM = pl.BlockSpec(memory_space=pltpu.VMEM)
DMA = pltpu.SemaphoreType.DMA
LIMIT = 48 * 1024 * 1024


def flip(index, mask):
    weight = 1
    result = index
    while weight <= mask:
        if mask & weight:
            result = result + weight - 2 * weight * lax.rem(index // weight, 2)
        weight *= 2
    return result


def greet(devices):
    barrier = pltpu.get_barrier_semaphore()
    for device in devices:
        pl.semaphore_signal(barrier, inc=1, device_id=device, device_id_type=MESH)
    pl.semaphore_wait(barrier, len(devices))


def send(src, dst, send_sem, recv_sem, device):
    copy = pltpu.make_async_remote_copy(
        src_ref=src, dst_ref=dst, send_sem=send_sem, recv_sem=recv_sem, device_id=device, device_id_type=MESH
    )
    copy.start()
    return copy


def piece(ref, index, size, base=0):
    return ref.at[pl.ds(pl.multiple_of(base + index * size, 8), size)]


def fold(bits, width):
    while width > 1:
        width //= 2
        bits = jnp.bitwise_xor(bits, jnp.right_shift(bits, width))
    return jnp.bitwise_and(bits, 1)


def sketch_kernel(
    scale, x_ref, s_ref, k_ref, g_ref, t_ref, out_ref, g_out, p_out,
    term, high, low, rows_ref, got_y, got_z, part, g_core, g_sum, g_chip,
    proj, p_core, p_sum, p_chip, send_sem, recv_sem,
):
    me, col = lax.axis_index("frames"), lax.axis_index("bins")
    core = lax.rem(col, 2)
    side = (flip(me, 1), col)
    near = (flip(me, 2), col)
    far = (flip(me, 4), col)
    sibling = (me, flip(col, 1))
    across = (me, flip(col, 2))
    greet([side, near, far, sibling, across])
    half = g_ref.shape[0] // 2
    gram_1 = send(piece(g_ref, 1 - core, half), g_core, send_sem.at[14], recv_sem.at[14], sibling)
    frame_rows = x_ref.shape[0]
    outer = frame_rows // SIDE
    tile = 128
    span = k_ref.shape[0] // 2
    share = span // 2
    spans = [pl.ds(0, span), pl.ds(span, span)]
    value = x_ref[...]
    rounded = value.astype(jnp.bfloat16)
    high[...] = rounded
    low[...] = (value - rounded.astype(jnp.float32)).astype(jnp.bfloat16)

    def compute(r, h):
        odd = 0
        for bit in range(3):
            if not r >> bit & 1:
                odd = odd + lax.rem(me // (1 << bit), 2)

        def step(index, carry):
            where = pl.ds(pl.multiple_of(h * span + index * tile, tile), tile)
            kept = k_ref[where, r : r + 1]
            lane = lax.broadcasted_iota(jnp.int32, (tile, SIDE), 1)
            bits = fold(jnp.bitwise_and(kept, lane), SIDE.bit_length() - 1)
            table = (1 - 2 * jnp.bitwise_and(bits + odd, 1)).astype(jnp.float32)
            upper = jnp.right_shift(kept, 8)
            for a in range(outer):
                sign = (1 - 2 * fold(jnp.bitwise_and(upper, a), 8)).astype(jnp.float32)
                cols = slice(a * SIDE, (a + 1) * SIDE)
                flips = (1 - 2 * s_ref[:, cols]).astype(jnp.float32)
                rows_ref[:, cols] = ((table * sign) * flips).astype(jnp.bfloat16)
            rows = rows_ref[...]
            term[r, where] = jnp.dot(rows, high[...], preferred_element_type=jnp.float32) + jnp.dot(
                rows, low[...], preferred_element_type=jnp.float32
            )
            return carry

        lax.fori_loop(0, span // tile, step, 0)

    copies = []

    def go(src, dst, n, device):
        copies.append(send(src, dst, send_sem.at[n], recv_sem.at[n], device))
        return copies[-1]

    by_y, first, second, third, proj_1, proj_2, proj_3 = ({} for _ in range(7))

    def odd_terms(h):
        for z in (3, 2, 1, 0):
            compute(2 * z + 1, h)
            by_y[h, z] = go(term.at[2 * z + 1, spans[h]], got_y.at[z, spans[h]], 4 * h + z, side)

    def to_near(h):
        by_y[h, 3].wait_recv()
        part[0, spans[h]] = term[6, spans[h]] + got_y[3, spans[h]]
        first[h] = go(part.at[0, spans[h]], got_z.at[0, spans[h]], 8 + 3 * h, near)

    def to_far(h):
        by_y[h, 2].wait_recv()
        first[h].wait_recv()
        part[1, spans[h]] = term[4, spans[h]] + got_y[2, spans[h]] + got_z[0, spans[h]]
        second[h] = go(part.at[1, spans[h]], got_z.at[1, spans[h]], 9 + 3 * h, far)

    def last_near(h):
        by_y[h, 1].wait_recv()
        part[2, spans[h]] = term[2, spans[h]] + got_y[1, spans[h]]
        third[h] = go(part.at[2, spans[h]], got_z.at[2, spans[h]], 10 + 3 * h, near)

    def split(value):
        top = value.astype(jnp.bfloat16)
        return top, (value - top.astype(jnp.float32)).astype(jnp.bfloat16)

    def finish(h):
        here = spans[h]
        by_y[h, 0].wait_recv()
        third[h].wait_recv()
        second[h].wait_recv()
        sketch = ((term[0, here] + got_y[0, here]) + (got_z[2, here] + got_z[1, here])) * scale
        out_ref[here] = sketch
        s_high, s_low = split(sketch)
        t_high, t_low = split(t_ref[...])

        def dot(left, right):
            return lax.dot_general(left, right, (((1,), (1,)), ((), ())), preferred_element_type=jnp.float32)

        proj[here] = dot(s_high, t_high) + (dot(s_high, t_low) + dot(s_low, t_high))
        theirs = piece(proj, 1 - core, share, h * span)
        proj_1[h] = go(theirs, p_core.at[h], 17 + 3 * h, sibling)

    def proj_across(h):
        proj_1[h].wait_recv()
        p_sum[h] = piece(proj, core, share, h * span)[...] + p_core[h]
        proj_2[h] = go(p_sum.at[h], p_chip.at[h], 18 + 3 * h, across)

    def proj_back(h):
        proj_2[h].wait_recv()
        mine = piece(p_out, core, share, h * span)
        mine[...] = p_sum[h] + p_chip[h]
        proj_3[h] = go(mine, mine, 19 + 3 * h, sibling)

    odd_terms(0)
    gram_1.wait_recv()
    g_sum[...] = piece(g_ref, core, half)[...] + g_core[...]
    gram_2 = go(g_sum, g_chip, 15, across)
    compute(6, 0)
    to_near(0)
    compute(4, 0)
    odd_terms(1)
    to_far(0)
    compute(2, 0)
    compute(0, 0)
    last_near(0)
    gram_2.wait_recv()
    mine = piece(g_out, core, half)
    mine[...] = g_sum[...] + g_chip[...]
    gram_3 = go(mine, mine, 16, sibling)
    for r in (6, 4, 2, 0):
        compute(r, 1)
    finish(0)
    to_near(1)
    proj_across(0)
    to_far(1)
    proj_back(0)
    last_near(1)
    finish(1)
    proj_across(1)
    proj_back(1)
    gram_3.wait_recv()
    for h in (0, 1):
        proj_3[h].wait_recv()
    for copy in (gram_1, *copies):
        copy.wait_send()


def make_sketch(spectrum, sign_row, kept, gram, templates, scale):
    frame_rows, cols = spectrum.shape
    rows = kept.shape[0]
    parts = templates.shape[0]
    half = (gram.shape[0] // 2, gram.shape[1])
    f32, bf16 = jnp.float32, jnp.bfloat16
    return pl.pallas_call(
        lambda *refs: sketch_kernel(scale, *refs),
        out_shape=(jax.ShapeDtypeStruct((rows, cols), f32), jax.ShapeDtypeStruct(gram.shape, f32), jax.ShapeDtypeStruct((rows, parts), f32)),
        in_specs=[VMEM] * 5,
        out_specs=(VMEM, VMEM, VMEM),
        scratch_shapes=[
            pltpu.VMEM((8, rows, cols), f32),
            pltpu.VMEM((frame_rows, cols), bf16),
            pltpu.VMEM((frame_rows, cols), bf16),
            pltpu.VMEM((128, frame_rows), bf16),
            pltpu.VMEM((4, rows, cols), f32),
            pltpu.VMEM((3, rows, cols), f32),
            pltpu.VMEM((3, rows, cols), f32),
            pltpu.VMEM(half, f32),
            pltpu.VMEM(half, f32),
            pltpu.VMEM(half, f32),
            pltpu.VMEM((rows, parts), f32),
            pltpu.VMEM((2, rows // 4, parts), f32),
            pltpu.VMEM((2, rows // 4, parts), f32),
            pltpu.VMEM((2, rows // 4, parts), f32),
            DMA((23,)),
            DMA((23,)),
        ],
        compiler_params=pltpu.CompilerParams(collective_id=0, has_side_effects=True, vmem_limit_bytes=LIMIT),
        name="make_sketch",
    )(spectrum, sign_row, kept, gram, templates)


def bins_kernel(count, *refs):
    ins, outs = refs[:count], refs[count : 2 * count]
    from_core, sums, from_chip = (refs[(2 + i) * count : (3 + i) * count] for i in range(3))
    send_sem, recv_sem = refs[5 * count :]
    row, me = lax.axis_index("frames"), lax.axis_index("bins")
    core = lax.rem(me, 2)
    sibling = (row, flip(me, 1))
    across = (row, flip(me, 2))
    greet([sibling, across])
    cuts = []
    for k in range(count):
        half = ins[k].shape[0] // 2
        size = half // 2
        for part in range(2):
            cuts.append((k, half, part * size, size))
    stage_1, stage_2, stage_3 = [], [], []
    for n, (k, half, start, size) in enumerate(cuts):
        theirs = ins[k].at[pl.ds(pl.multiple_of((1 - core) * half + start, 8), size)]
        got = from_core[k].at[pl.ds(start, size)]
        stage_1.append(send(theirs, got, send_sem.at[n], recv_sem.at[n], sibling))
    for n, (k, half, start, size) in enumerate(cuts):
        stage_1[n].wait_recv()
        here = pl.ds(start, size)
        sums[k][here] = ins[k][pl.ds(pl.multiple_of(core * half + start, 8), size)] + from_core[k][here]
        stage_2.append(send(sums[k].at[here], from_chip[k].at[here], send_sem.at[8 + n], recv_sem.at[8 + n], across))
    for n, (k, half, start, size) in enumerate(cuts):
        stage_2[n].wait_recv()
        here = pl.ds(start, size)
        mine = outs[k].at[pl.ds(pl.multiple_of(core * half + start, 8), size)]
        mine[...] = sums[k][here] + from_chip[k][here]
        stage_3.append(send(mine, mine, send_sem.at[16 + n], recv_sem.at[16 + n], sibling))
    for copy in stage_3:
        copy.wait_recv()
    for copy in (*stage_1, *stage_2, *stage_3):
        copy.wait_send()


def sum_bins(name, collective_id, *arrays):
    f32 = jnp.float32
    count = len(arrays)
    halves = [(array.shape[0] // 2, array.shape[1]) for array in arrays]
    return pl.pallas_call(
        lambda *refs: bins_kernel(count, *refs),
        out_shape=tuple(jax.ShapeDtypeStruct(array.shape, f32) for array in arrays),
        in_specs=[VMEM] * count,
        out_specs=(VMEM,) * count,
        scratch_shapes=[pltpu.VMEM(shape, f32) for _ in range(3) for shape in halves] + [DMA((24,)), DMA((24,))],
        compiler_params=pltpu.CompilerParams(collective_id=collective_id, has_side_effects=True, vmem_limit_bytes=LIMIT),
        name=name,
    )(*arrays)


def pack(gram, packed):
    n = packed.shape[0] // 2
    packed[:n] = gram[:n]
    packed[n:, : 2 * n] = gram[n : 2 * n, n:]
    packed[n:, 2 * n :] = gram[2 * n :, 2 * n :]


def unpack(packed, gram):
    n = packed.shape[0] // 2
    gram[:n] = packed[:n]
    gram[n : 2 * n, :n] = packed[:n, n : 2 * n].T
    gram[2 * n :, :n] = packed[:n, 2 * n :].T
    gram[n : 2 * n, n:] = packed[n:, : 2 * n]
    gram[2 * n :, n : 2 * n] = packed[n:, n : 2 * n].T
    gram[2 * n :, 2 * n :] = packed[n:, 2 * n :]


def frames_kernel(
    g_ref, c_ref, g_full, c_out, g_y, c_y, g_z, c_z, g_part, c_part, g_in, g_out, send_sem, recv_sem
):
    me, col = lax.axis_index("frames"), lax.axis_index("bins")
    core = lax.rem(col, 2)
    side = (flip(me, 1), col)
    peers = {z: (flip(me, 2 * z), col) for z in (3, 2, 1)}
    sibling = (me, flip(col, 1))
    pack(g_ref, g_in)
    greet([side, *peers.values(), sibling])
    g_half = g_in.shape[0] // 2
    arrays = (
        (0, g_in.at[pl.ds(pl.multiple_of(core * g_half, 8), g_half)], g_half // 8, g_y, g_z, g_part, g_out, core * g_half),
        (16, c_ref, c_ref.shape[0] // 8, c_y, c_z, c_part, c_out, 0),
    )
    copies = []

    def go(src, dst, n, device):
        copies.append(send(src, dst, send_sem.at[n], recv_sem.at[n], device))
        return copies[-1]

    by_y, by_z, back, passed = {}, {}, {}, {}
    for k, src, size, from_y, from_z, part, out, base in arrays:
        for z in (3, 2, 1, 0):
            by_y[k, z] = go(piece(src, flip(me, 2 * z + 1), size), from_y.at[z], k + z, side)
    for k, src, size, from_y, from_z, part, out, base in arrays:
        for z in (3, 2, 1):
            by_y[k, z].wait_recv()
            part[z - 1] = piece(src, flip(me, 2 * z), size)[...] + from_y[z]
            by_z[k, z] = go(part.at[z - 1], from_z.at[z - 1], k + 4 + z, peers[z])
    for k, src, size, from_y, from_z, part, out, base in arrays:
        by_y[k, 0].wait_recv()
        total = piece(src, me, size)[...] + from_y[0]
        for z in (1, 2, 3):
            by_z[k, z].wait_recv()
            total = total + from_z[z - 1]
        mine = piece(out, me, size, base)
        mine[...] = total
        for z in (3, 2, 1):
            back[k, z] = go(mine, mine, k + 8 + z, peers[z])
        back[k, 0] = go(mine, mine, k + 8, side)
    for k, src, size, from_y, from_z, part, out, base in arrays:
        for z in (1, 2, 3):
            back[k, z].wait_recv()
            theirs = piece(out, flip(me, 2 * z), size, base)
            passed[k, z] = go(theirs, theirs, k + 12 + z, side)
        if k == 0:
            back[k, 0].wait_recv()
            for z in (1, 2, 3):
                passed[k, z].wait_recv()
            mine = piece(g_out, core, g_half)
            swap = go(mine, mine, 12, sibling)
    back[16, 0].wait_recv()
    for z in (1, 2, 3):
        passed[16, z].wait_recv()
    swap.wait_recv()
    unpack(g_out, g_full)
    for copy in copies:
        copy.wait_send()


def sum_frames(gram, cross):
    f32 = jnp.float32
    parts, cols = cross.shape
    packed = (2 * gram.shape[0] // 3, gram.shape[1])
    g_piece = (packed[0] // 16, packed[1])
    c_piece = (parts // 8, cols)
    return pl.pallas_call(
        frames_kernel,
        out_shape=(
            jax.ShapeDtypeStruct(gram.shape, f32),
            jax.ShapeDtypeStruct(cross.shape, f32),
        ),
        in_specs=[VMEM, VMEM],
        out_specs=(VMEM, VMEM),
        scratch_shapes=[pltpu.VMEM((count, *shape), f32) for count in (4, 3, 3) for shape in (g_piece, c_piece)]
        + [pltpu.VMEM(packed, f32), pltpu.VMEM(packed, f32), DMA((32,)), DMA((32,))],
        compiler_params=pltpu.CompilerParams(collective_id=2, has_side_effects=True, vmem_limit_bytes=LIMIT),
        name="sum_frames",
    )(gram, cross)


def body_8x4(spectrum, sign_bits, kept_rows, mask, w_init, h_init):
    damping = 1.0
    high = lax.Precision.HIGH
    block_count = 8
    position = lax.axis_index("frames")
    frame_rows, cols = spectrum.shape
    per_block = kept_rows.shape[0] // block_count
    parts = w_init.shape[1]
    padded = -(-parts // 128) * 128
    templates = jnp.pad(h_init * mask.astype(jnp.float32), ((0, padded - parts), (0, 0)))
    activations = jnp.pad(w_init, ((0, 0), (0, padded - parts)))
    blocks = jnp.bitwise_xor(position, jnp.arange(block_count, dtype=jnp.int32))
    kept = jnp.take(kept_rows.reshape(block_count, per_block), blocks, axis=0, mode="clip").T
    sketch, gram_h, proj = make_sketch(
        spectrum,
        sign_bits.reshape(1, frame_rows),
        kept,
        jnp.dot(templates, templates.T, precision=high),
        templates,
        1.0 / (frame_rows * block_count) ** 0.5,
    )
    for round_index in range(ITERS):
        if round_index:
            gram_h, proj = sum_bins(
                "sum_bins",
                1,
                jnp.dot(templates, templates.T, precision=high),
                jnp.dot(sketch, templates.T, precision=high),
            )
        lower = jnp.maximum(-proj, 0.0) + jnp.dot(activations, gram_h, precision=high) + damping
        activations = activations * jnp.sqrt((jnp.maximum(proj, 0.0) + damping) / lower)
        gram_w, cross = sum_frames(
            jnp.dot(activations.T, activations, precision=high),
            jnp.dot(activations.T, sketch, precision=high),
        )
        lower = jnp.maximum(-cross, 0.0) + jnp.dot(gram_w, templates, precision=high) + damping
        templates = templates * jnp.sqrt((jnp.maximum(cross, 0.0) + damping) / lower)
    return (activations[:, :parts], templates[:parts])


def solution(mesh):
    in_specs = (
        P("frames", "bins"),
        P("frames"),
        P(),
        P(None, "bins"),
        P("frames", None),
        P(None, "bins"),
    )
    out_specs = (P("frames", None), P(None, "bins"))
    small = mesh.shape["frames"] == 8 and mesh.shape["bins"] == 4
    return jax.shard_map(body_8x4 if small else body, mesh=mesh, in_specs=in_specs, out_specs=out_specs, check_vma=False)
```
